128 devices in a mesh: dp: 4 (over y_hi, core), owner: 32 (over z, y_lo, x).
Axes of the slice: x: 4, y: 4 (y_hi: 2, y_lo: 2; y = y_hi * 2 + y_lo), z: 4, core: 2. Of those that a mesh axis runs over, the one named last changes fastest.
Arguments:
- stats: bfloat16 [32, 2, 8192, 768], P('owner', None, 'dp'), may hold values from -6 to 6
- damping: float32 [32, 2], P('owner'), may hold values from 0.1 to 1
- grad: bfloat16 [32, 768, 4, 768], P('owner', 'dp'), may hold values from -6 to 6
Outputs:
- precond: bfloat16 [32, 768, 4, 768], P('owner', 'dp')
The draws below stay inside these ranges and needn't reach their ends.
All inputs are finite; a program needn't handle non-finite values. Where the reference program divides by a largest or mean magnitude, that divisor is 1e-20 or more.
Results may differ from the reference program's by a relative error of at most 0.0063.
Values may be sent and summed in bfloat16 or wider, within the bound.
A program may use at most 128 MiB of HBM per device.

```python
import math
import jax
import jax.numpy as jnp
from jax import lax

B = 768
ITERS = 5
S = 4
OWNERS = 32
TOKENS = 8192


def block_levels(rng, extent, shards, low, high):
    def one(position, blocks):
        steps = jax.random.uniform(jax.random.fold_in(jax.random.fold_in(rng, 6), position), (blocks,), jnp.float32, low / len(shards), high / len(shards))
        return jnp.repeat(jnp.exp(steps), extent[position] // blocks).reshape((-1,) + (1,) * (len(extent) - position - 1))

    gain = one(*shards[0])
    for cut in shards[1:]:
        gain = gain * one(*cut)
    return gain


def gaussian(stream_key, shape, deviation, reach, split=(), kind=jnp.bfloat16):
    drawn = deviation * jax.random.normal(stream_key, shape, jnp.float32)
    if split:
        drawn = drawn * block_levels(stream_key, shape, split, -0.22, 0.18)
    return jnp.clip(drawn, -reach, reach).astype(kind)


def setup_inputs(seed: int = 0) -> dict:
    keys = jax.random.split(jax.random.key(seed), 4)
    stats = gaussian(keys[0], (OWNERS, 2, TOKENS, B), 1.0, 6.0, ((0, 32), (2, 4)))
    damping = jnp.clip(jnp.exp(math.log(1.0) - 2.3025851 * jax.random.uniform(keys[1], (OWNERS, 2), jnp.float32) ** block_levels(keys[1], (OWNERS, 2), ((0, 32),), -0.2, 0.2)), 0.1, 1.0)
    grad = gaussian(keys[2], (OWNERS, B, S, B), 1.0, 6.0, ((0, 32), (1, 4)))
    return dict(stats=stats, damping=damping, grad=grad)


HIGH = lax.Precision.HIGHEST


def invert_block(data, lam):
    cov = lax.dot_general(data, data, (((0,), (0,)), ((), ())), preferred_element_type=jnp.float32) / TOKENS
    eye = jnp.eye(B, dtype=jnp.float32)
    matrix = cov + lam * eye
    factor = 1.0 / jnp.max(jnp.sum(jnp.abs(matrix), axis=1))
    iterate = eye * factor
    for step in range(ITERS):
        product = jnp.dot(matrix, iterate, precision=HIGH, preferred_element_type=jnp.float32)
        iterate = 2.0 * iterate - jnp.dot(iterate, product, precision=HIGH, preferred_element_type=jnp.float32)
    return iterate.astype(jnp.bfloat16)


def invert_row(pair):
    data, lam = pair
    first = invert_block(data[0], lam[0])
    second = invert_block(data[1], lam[1])
    return jnp.stack([first, second], axis=0)


def precondition(pack):
    tiles, right_inv, left_inv = pack
    right_part = jnp.einsum("rtc,tcd->rtd", tiles.astype(jnp.float32), right_inv.astype(jnp.float32)).astype(jnp.bfloat16)
    return jnp.einsum("ir,rtd->itd", left_inv.astype(jnp.float32), right_part.astype(jnp.float32)).astype(jnp.bfloat16)


def reference(stats, damping, grad):
    inverses = lax.map(invert_row, (stats, damping))
    a_inv = inverses[:, 0]
    g_inv = inverses[:, 1]
    shifted = jnp.stack([jnp.roll(a_inv, t, axis=0) for t in range(S)], axis=1)
    return lax.map(precondition, (grad, shifted, g_inv))
```

```python
import jax
import jax.numpy as jnp
from jax import lax
from jax.experimental import pallas as pl
from jax.experimental.pallas import tpu as pltpu
from jax.sharding import PartitionSpec as P

MESH = pl.DeviceIdType.MESH
F32 = jnp.float32
BF16 = jnp.bfloat16
N = 256
W = 768
PAIRS = ((0, 0), (0, 1), (0, 2), (1, 1), (1, 2), (2, 2))
TAIL = len(PAIRS) * N
ROWS = TAIL + 16
CHUNKS = ((0, 512), (512, 512), (1024, 528))
CHUNK_PAIRS = ((0, 1), (2, 3), (4, 5))
TOKEN_CHUNK = 1024


def eye_mask():
    shape = (N, N)
    return lax.broadcasted_iota(jnp.int32, shape, 0) == lax.broadcasted_iota(jnp.int32, shape, 1)


def gram(a, b):
    return lax.dot_general(a, b, (((0,), (0,)), ((), ())), preferred_element_type=F32)


def pack_diagonal(diags):
    row = lax.broadcasted_iota(jnp.int32, (16, N), 0)
    out = jnp.zeros((16, N), F32)
    for i, d in enumerate(diags):
        high = d.astype(BF16).astype(F32)
        out = jnp.where(row == i, high, out)
        out = jnp.where(row == i + 3, d - high, out)
    return out.astype(BF16)


def unpack_diagonal(tail):
    t = tail.astype(F32)
    return [t[i : i + 1] + t[i + 3 : i + 4] for i in range(3)]


def invert(packed, tokens, off_r, off_s, r_mat, s_mat, result):
    eye = eye_mask()
    diag = [d * (1.0 / tokens) for d in unpack_diagonal(packed[TAIL:ROWS, :])]
    sums = [None] * 3

    def add(i, v):
        sums[i] = v if sums[i] is None else sums[i] + v

    for b, (i, j) in enumerate(PAIRS):
        v = packed[b * N : (b + 1) * N, :].astype(F32) * (1.0 / tokens)
        if i == j:
            v = jnp.where(eye, 0.0, v)
        a = jnp.abs(v)
        add(j, jnp.sum(a, axis=0, keepdims=True))
        if i != j:
            add(i, jnp.sum(a.T, axis=0, keepdims=True))
    sums = [s + jnp.abs(d) for s, d in zip(sums, diag)]
    factor = 1.0 / jnp.max(jnp.maximum(jnp.maximum(sums[0], sums[1]), sums[2]))
    d_row = [1.0 - factor * d for d in diag]
    d_col = [
        jnp.sum(jnp.where(eye, jnp.broadcast_to(d, (N, N)), 0.0), axis=1, keepdims=True)
        for d in d_row
    ]

    def put(ref, i, j, v):
        ref[i * N : (i + 1) * N, j * N : (j + 1) * N] = v.astype(BF16)
        if i != j:
            ref[j * N : (j + 1) * N, i * N : (i + 1) * N] = v.T.astype(BF16)

    scale = factor * (-1.0 / tokens)
    for b, (i, j) in enumerate(PAIRS):
        v = packed[b * N : (b + 1) * N, :].astype(F32) * scale
        if i == j:
            v = jnp.where(eye, 0.0, v)
        off_r[b] = v
        off_s[b] = v
        put(r_mat.at[0], i, j, v)
    s_row = [1.0 + d for d in d_row]
    s_col = [1.0 + d for d in d_col]

    def product(a, b, i, j):
        return jnp.dot(
            a[i * N : (i + 1) * N, :], b[:, j * N : (j + 1) * N], preferred_element_type=F32
        )

    def square(src, dst):
        for b, (i, j) in enumerate(PAIRS):
            v = off_r[b] * (d_col[i] + d_row[j]) + product(src, src, i, j)
            off_r[b] = v
            put(dst, i, j, v)

    square(r_mat.at[0], r_mat.at[1])
    d_row = [d * d for d in d_row]
    d_col = [d * d for d in d_col]
    now = 1
    left = r_mat.at[0]
    for k in range(4):
        last = k == 3
        for b, (i, j) in enumerate(PAIRS):
            v = s_col[i] * off_r[b] + off_s[b] * (1.0 + d_row[j])
            v = v + product(left, r_mat.at[now], i, j)
            if last:
                if i == j:
                    v = v + jnp.where(eye, s_row[j] * (1.0 + d_row[j]), 0.0)
                put(result, i, j, v * factor)
            else:
                off_s[b] = v
                put(s_mat.at[k % 2], i, j, v)
        if not last:
            s_row = [s * (1.0 + d) for s, d in zip(s_row, d_row)]
            s_col = [s * (1.0 + d) for s, d in zip(s_col, d_col)]
            left = s_mat.at[k % 2]
            square(r_mat.at[now], r_mat.at[3 - now])
            now = 3 - now
            d_row = [d * d for d in d_row]
            d_col = [d * d for d in d_col]


def kernel(
    tokens,
    damping,
    stats,
    grad,
    out,
    sbuf,
    partner_acc,
    own_acc,
    partner_in,
    y_out,
    y_in,
    packed,
    off_r,
    off_s,
    r_mat,
    s_mat,
    inverse,
    g_rows,
    g_buf,
    q_buf,
    o_buf,
    stats_sem,
    local_sem,
    grad_send,
    grad_recv,
    part_send,
    part_recv,
    y_send,
    y_recv,
    x_send,
    x_recv,
    g_send,
    g_recv,
    out_send,
    out_recv,
):
    dp = lax.axis_index("dp")
    o = lax.axis_index("owner")
    h, c = dp // 2, dp % 2
    x = o % 4
    quarter = W // 4
    half = W // 2

    def ring(t):
        return o - x + (x + t) % 4

    next_row = (o + 4) % 32
    prev_row = (o + 28) % 32
    partner = (h * 2 + 1 - c, o)
    across = ((1 - h) * 2 + c, o)

    loads = []
    steps = sbuf.shape[1] // TOKEN_CHUNK
    for j in range(2):
        f = (1 - c) if j == 0 else c
        for k in range(steps):
            rows = pl.ds(k * TOKEN_CHUNK, TOKEN_CHUNK)
            cp = pltpu.make_async_copy(
                stats.at[f, rows], sbuf.at[j, rows], stats_sem.at[j * steps + k]
            )
            cp.start()
            loads.append(cp)
    mine = pl.ds(pl.multiple_of(dp * quarter, quarter), quarter)
    local = []
    for tau in range(2):
        cp = pltpu.make_async_copy(grad.at[2 * c + tau], g_buf.at[tau, mine], local_sem.at[tau])
        cp.start()
        local.append(cp)

    barrier = pltpu.get_barrier_semaphore()

    def greet(device):
        pl.semaphore_signal(barrier, inc=1, device_id=device, device_id_type=MESH)

    greet(partner)
    greet(across)
    greet(((1 - h) * 2 + 1 - c, o))

    @pl.when(c == 0)
    def _():
        greet((dp, ring(1)))
        greet((dp, ring(3)))
        greet((dp + 1, ring(2)))
        greet((dp + 1, ring(3)))
        greet((dp, next_row))
        greet((dp, prev_row))
        pl.semaphore_wait(barrier, 9)

    @pl.when(c == 1)
    def _():
        greet((dp - 1, ring(2)))
        greet((dp - 1, ring(1)))
        pl.semaphore_wait(barrier, 5)

    def grad_copy(rel, tau):
        to_h = h if rel < 2 else 1 - h
        to_c = c if rel % 2 == 0 else 1 - c
        n = (rel - 1) * 2 + tau
        return pltpu.make_async_remote_copy(
            src_ref=grad.at[2 * to_c + tau],
            dst_ref=g_buf.at[tau, mine],
            send_sem=grad_send.at[n],
            recv_sem=grad_recv.at[n],
            device_id=(to_h * 2 + to_c, o),
            device_id_type=MESH,
        )

    grad_copy(2, 0).start()

    def partial(j, acc):
        for k in range(steps):
            loads[j * steps + k].wait()
            rows = slice(k * TOKEN_CHUNK, (k + 1) * TOKEN_CHUNK)
            for i in range(3):
                r = gram(sbuf[j, rows, i * N : (i + 1) * N], sbuf[j, rows, i * N :])
                for jj in range(i, 3):
                    b = PAIRS.index((i, jj))
                    v = r[:, (jj - i) * N : (jj - i + 1) * N]
                    if k == 0:
                        acc[b] = v
                    else:
                        acc[b] += v

    part_copies = [
        pltpu.make_async_remote_copy(
            src_ref=partner_acc.at[pl.ds(3 * k, 3)],
            dst_ref=partner_in.at[pl.ds(3 * k, 3)],
            send_sem=part_send.at[k],
            recv_sem=part_recv.at[k],
            device_id=partner,
            device_id_type=MESH,
        )
        for k in range(2)
    ]
    partial(0, partner_acc)
    for cp in part_copies:
        cp.start()
    partial(1, own_acc)

    grad_copy(1, 0).start()
    grad_copy(1, 1).start()

    eye = eye_mask()

    def y_copy(k):
        start, size = CHUNKS[k]
        return pltpu.make_async_remote_copy(
            src_ref=y_out.at[pl.ds(start, size)],
            dst_ref=y_in.at[pl.ds(start, size)],
            send_sem=y_send.at[k],
            recv_sem=y_recv.at[k],
            device_id=across,
            device_id_type=MESH,
        )

    diags = []
    for k in range(3):
        for b in CHUNK_PAIRS[k]:
            if b % 3 == 0:
                part_copies[b // 3].wait_recv()
            v = own_acc[b] + partner_in[b]
            own_acc[b] = v
            y_out[b * N : (b + 1) * N, :] = v.astype(BF16)
            if PAIRS[b][0] == PAIRS[b][1]:
                diags.append(jnp.sum(jnp.where(eye, v, 0.0), axis=0, keepdims=True))
        if k == 2:
            y_out[TAIL:ROWS, :] = pack_diagonal(diags)
        y_copy(k).start()

    def x_copy(t, k, slot):
        start, size = CHUNKS[k]
        to_slot = (2, 1, 1, 2)[t]
        device = (dp, next_row) if t == 0 else (dp + (0 if t == 1 else 1), ring(t))
        return pltpu.make_async_remote_copy(
            src_ref=packed.at[slot, pl.ds(start, size)],
            dst_ref=packed.at[to_slot, pl.ds(start, size)],
            send_sem=x_send.at[t * 3 + k],
            recv_sem=x_recv.at[to_slot * 3 + k],
            device_id=device,
            device_id_type=MESH,
        )

    lam = damping[c] * tokens
    for k in range(3):
        y_copy(k).wait_recv()
        for b in CHUNK_PAIRS[k]:
            rows = slice(b * N, (b + 1) * N)
            packed[0, rows, :] = (own_acc[b] + y_in[rows, :].astype(F32)).astype(BF16)
        if k == 2:
            other = unpack_diagonal(y_in[TAIL:ROWS, :])
            packed[0, TAIL:ROWS, :] = pack_diagonal([d + e + lam for d, e in zip(diags, other)])

        @pl.when((c == 0) & (x >= 1))
        def _():
            x_copy(0, k, 0).start()

        for t in range(1, 4):

            @pl.when((c == 0) & (x + t < 4))
            def _():
                x_copy(t, k, 0).start()

    for k in range(3):
        y_copy(k).wait_send()
    grad_copy(3, 0).start()
    grad_copy(2, 1).start()
    grad_copy(3, 1).start()

    @pl.when((c == 0) & (x >= 1))
    def _():
        for k in range(3):
            x_copy(0, k, 0).wait_recv()
            for t in range(1, 4):

                @pl.when(x + t >= 4)
                def _():
                    x_copy(t, k, 2).start()

    g_copy = pltpu.make_async_remote_copy(
        src_ref=g_rows,
        dst_ref=g_rows,
        send_sem=g_send.at[0],
        recv_sem=g_recv.at[0],
        device_id=partner,
        device_id_type=MESH,
    )
    chip_rows = pl.ds(pl.multiple_of(h * half, half), half)

    def one(n, _):
        @pl.when((c == 1) | (n < 2))
        def _():
            @pl.when(n == 1)
            def _():
                for k in range(3):
                    x_copy(1, k, 0).wait_recv()

            @pl.when(n == 2)
            def _():
                for k in range(3):
                    x_copy(3, k, 0).wait_recv()

            invert(packed.at[n], tokens, off_r, off_s, r_mat, s_mat, inverse.at[n])

            @pl.when((c == 1) & (n == 0))
            def _():
                g_rows[...] = inverse[0, chip_rows, :]
                g_copy.start()

        return 0

    lax.fori_loop(0, 3, one, 0)

    @pl.when(c == 0)
    def _():
        g_copy.wait_recv()

    own_rows = pl.ds(pl.multiple_of(c * quarter, quarter), quarter)
    other_rows = pl.ds(pl.multiple_of((1 - c) * quarter, quarter), quarter)

    def out_copy(tau):
        return pltpu.make_async_remote_copy(
            src_ref=o_buf.at[tau],
            dst_ref=out.at[2 * c + tau],
            send_sem=out_send.at[tau],
            recv_sem=out_recv.at[tau],
            device_id=partner,
            device_id_type=MESH,
        )

    for tau in range(2):
        local[tau].wait()
        for rel in (1, 2, 3):
            grad_copy(rel, tau).wait_recv()
        q_buf[...] = jnp.dot(g_rows[...], g_buf[tau], preferred_element_type=F32).astype(BF16)
        a = inverse.at[tau + c]
        o_buf[tau] = jnp.dot(q_buf[other_rows, :], a[...], preferred_element_type=F32).astype(BF16)
        out_copy(tau).start()
        out[2 * c + tau] = jnp.dot(q_buf[own_rows, :], a[...], preferred_element_type=F32).astype(
            BF16
        )

    for cp in part_copies:
        cp.wait_send()
    for rel in (1, 2, 3):
        for tau in range(2):
            grad_copy(rel, tau).wait_send()

    @pl.when(c == 1)
    def _():
        g_copy.wait_send()

    @pl.when(c == 0)
    def _():
        for k in range(3):

            @pl.when(x >= 1)
            def _():
                x_copy(0, k, 0).wait_send()

            for t in range(1, 4):
                x_copy(t, k, 0).wait_send()

    for tau in range(2):
        out_copy(tau).wait()


def per_device(stats, damping, grad, total_tokens):
    local_tokens = stats.shape[2]
    quarter, band, width = grad.shape[1:]
    tiles = jnp.swapaxes(grad[0], 0, 1)
    dma = pltpu.SemaphoreType.DMA
    import functools

    result = pl.pallas_call(
        functools.partial(kernel, float(total_tokens)),
        out_shape=jax.ShapeDtypeStruct((band, quarter, width), BF16),
        in_specs=[
            pl.BlockSpec(memory_space=pltpu.SMEM),
            pl.BlockSpec(memory_space=pl.ANY),
            pl.BlockSpec(memory_space=pl.ANY),
        ],
        out_specs=pl.BlockSpec(memory_space=pltpu.VMEM),
        scratch_shapes=[
            pltpu.VMEM((2, local_tokens, width), BF16),
            pltpu.VMEM((6, N, N), F32),
            pltpu.VMEM((6, N, N), F32),
            pltpu.VMEM((6, N, N), F32),
            pltpu.VMEM((ROWS, N), BF16),
            pltpu.VMEM((ROWS, N), BF16),
            pltpu.VMEM((3, ROWS, N), BF16),
            pltpu.VMEM((6, N, N), F32),
            pltpu.VMEM((6, N, N), F32),
            pltpu.VMEM((3, W, W), BF16),
            pltpu.VMEM((2, W, W), BF16),
            pltpu.VMEM((3, W, W), BF16),
            pltpu.VMEM((W // 2, W), BF16),
            pltpu.VMEM((2, W, W), BF16),
            pltpu.VMEM((W // 2, W), BF16),
            pltpu.VMEM((2, W // 4, W), BF16),
            dma((2 * local_tokens // TOKEN_CHUNK,)),
            dma((2,)),
            dma((6,)),
            dma((6,)),
            dma((2,)),
            dma((2,)),
            dma((3,)),
            dma((3,)),
            dma((12,)),
            dma((9,)),
            dma((1,)),
            dma((1,)),
            dma((2,)),
            dma((2,)),
        ],
        compiler_params=pltpu.CompilerParams(
            collective_id=0, has_side_effects=True, vmem_limit_bytes=56 * 2**20
        ),
    )(damping[0], stats[0], tiles)
    return jnp.swapaxes(result, 0, 1)[None]


def solution(mesh):
    in_specs = (P("owner", None, "dp", None), P("owner", None), P("owner", "dp", None, None))
    out_specs = P("owner", "dp", None, None)

    def whole(stats, damping, grad):
        def one(s, d, g):
            return per_device(s, d, g, stats.shape[2])

        return jax.shard_map(
            one, mesh=mesh, in_specs=in_specs, out_specs=out_specs, check_vma=False
        )(stats, damping, grad)

    return whole
```

```python
import functools

import jax
import jax.numpy as jnp
from jax import lax
from jax.experimental import pallas as pl
from jax.experimental.pallas import tpu as pltpu
from jax.sharding import PartitionSpec as P

MESH = pl.DeviceIdType.MESH
F32 = jnp.float32
BF16 = jnp.bfloat16
N = 256
W = 768
PAIRS = ((0, 0), (0, 1), (0, 2), (1, 1), (1, 2), (2, 2))
H = N // 2
OFF = {(0, 1): 0, (0, 2): N, (1, 2): 2 * N}
UPPER = 3 * N
LOWER = UPPER + 3 * H
TAIL = LOWER + H + H // 2
ROWS = TAIL + 16
CHUNKS = tuple((k * N, N if k < 5 else ROWS - 5 * N) for k in range(6))
DATA = tuple((k * N, N if k < 5 else TAIL - 5 * N) for k in range(6))
TOKEN_CHUNK = 1024


def eye_mask():
    shape = (N, N)
    return lax.broadcasted_iota(jnp.int32, shape, 0) == lax.broadcasted_iota(jnp.int32, shape, 1)


def gram(a, b):
    return lax.dot_general(a, b, (((0,), (0,)), ((), ())), preferred_element_type=F32)


def pack_diagonal(diags):
    row = lax.broadcasted_iota(jnp.int32, (16, N), 0)
    out = jnp.zeros((16, N), F32)
    for i, d in enumerate(diags):
        high = d.astype(BF16).astype(F32)
        out = jnp.where(row == i, high, out)
        out = jnp.where(row == i + 5, d - high, out)
    return out.astype(BF16)


def unpack_diagonal(tail):
    t = tail.astype(F32)
    return [t[i : i + 1] + t[i + 5 : i + 6] for i in range(5)]


def add_block(acc, f, i, j, v, first):
    def put(rows, columns, w):
        if first:
            acc[f, rows, columns] = w
        else:
            acc[f, rows, columns] += w

    full = slice(0, N)
    if i != j:
        put(slice(OFF[i, j], OFF[i, j] + N), full, v)
        return
    put(slice(UPPER + i * H, UPPER + (i + 1) * H), full, v[:H])
    low = v[H:, H:]
    if i < 2:
        put(slice(LOWER, LOWER + H), slice(i * H, (i + 1) * H), low)
    else:
        rows = slice(LOWER + H, TAIL)
        put(rows, slice(0, H), low[: H // 2])
        put(rows, slice(H, N), low[H // 2 :])


def diagonals(k, v, bias):
    def pick(w, mask):
        return jnp.sum(jnp.where(mask, w + bias, 0.0), axis=0, keepdims=True)

    row = lax.broadcasted_iota(jnp.int32, (H, N), 0)
    lane = lax.broadcasted_iota(jnp.int32, (H, N), 1)
    if k == 3:
        return [pick(v[:H], row == lane), pick(v[H:], row == lane)]
    if k == 4:
        return [pick(v[:H], row == lane), pick(v[H:], row == lane % H)]
    if k == 5:
        row, lane = row[: H // 2], lane[: H // 2]
        return [pick(v, (lane == row) | (lane == row + H + H // 2))]
    return []


def invert(packed, tokens, off_r, off_s, r_mat, s_mat, result):
    eye = eye_mask()
    parts = [d * (1.0 / tokens) for d in unpack_diagonal(packed[TAIL:ROWS, :])]
    seconds = [parts[3][:, :H], parts[3][:, H:], parts[4][:, :H] + parts[4][:, H:]]
    diag = [jnp.concatenate([parts[i][:, :H], seconds[i]], axis=1) for i in range(3)]
    sums = [None] * 3

    def add(i, v):
        sums[i] = v if sums[i] is None else sums[i] + v

    def unpack(i, j):
        if i != j:
            return packed[OFF[i, j] : OFF[i, j] + N, :].astype(F32)
        top = packed[UPPER + i * H : UPPER + (i + 1) * H, :].astype(F32)
        if i < 2:
            low = packed[LOWER : LOWER + H, i * H : (i + 1) * H].astype(F32)
        else:
            both = packed[LOWER + H : TAIL, :].astype(F32)
            low = jnp.concatenate([both[:, :H], both[:, H:]], axis=0)
        bottom = jnp.concatenate([top[:, H:].T, low], axis=1)
        return jnp.concatenate([top, bottom], axis=0)

    for b, (i, j) in enumerate(PAIRS):
        v = unpack(i, j) * (1.0 / tokens)
        if i == j:
            v = jnp.where(eye, 0.0, v)
        off_r[b] = v
        a = jnp.abs(v)
        add(j, jnp.sum(a, axis=0, keepdims=True))
        if i != j:
            add(i, jnp.sum(a.T, axis=0, keepdims=True))
    sums = [s + jnp.abs(d) for s, d in zip(sums, diag)]
    factor = 1.0 / jnp.max(jnp.maximum(jnp.maximum(sums[0], sums[1]), sums[2]))
    d_row = [1.0 - factor * d for d in diag]
    d_col = [
        jnp.sum(jnp.where(eye, jnp.broadcast_to(d, (N, N)), 0.0), axis=1, keepdims=True)
        for d in d_row
    ]

    def put(ref, i, j, v):
        ref[i * N : (i + 1) * N, j * N : (j + 1) * N] = v.astype(BF16)
        if i != j:
            ref[j * N : (j + 1) * N, i * N : (i + 1) * N] = v.T.astype(BF16)

    for b, (i, j) in enumerate(PAIRS):
        v = off_r[b] * (-factor)
        off_r[b] = v
        off_s[b] = v
        put(r_mat.at[0], i, j, v)
    s_row = [1.0 + d for d in d_row]
    s_col = [1.0 + d for d in d_col]

    def product(a, b, i, j):
        return jnp.dot(
            a[i * N : (i + 1) * N, :], b[:, j * N : (j + 1) * N], preferred_element_type=F32
        )

    def square(src, dst):
        for b, (i, j) in enumerate(PAIRS):
            v = off_r[b] * (d_col[i] + d_row[j]) + product(src, src, i, j)
            off_r[b] = v
            put(dst, i, j, v)

    square(r_mat.at[0], r_mat.at[1])
    d_row = [d * d for d in d_row]
    d_col = [d * d for d in d_col]
    now = 1
    left = r_mat.at[0]
    for k in range(4):
        last = k == 3
        for b, (i, j) in enumerate(PAIRS):
            v = s_col[i] * off_r[b] + off_s[b] * (1.0 + d_row[j])
            v = v + product(left, r_mat.at[now], i, j)
            if last:
                if i == j:
                    v = v + jnp.where(eye, s_row[j] * (1.0 + d_row[j]), 0.0)
                put(result, i, j, v * factor)
            else:
                off_s[b] = v
                put(s_mat.at[k % 2], i, j, v)
        if not last:
            s_row = [s * (1.0 + d) for s, d in zip(s_row, d_row)]
            s_col = [s * (1.0 + d) for s, d in zip(s_col, d_col)]
            left = s_mat.at[k % 2]
            square(r_mat.at[now], r_mat.at[3 - now])
            now = 3 - now
            d_row = [d * d for d in d_row]
            d_col = [d * d for d in d_col]


def kernel(
    tokens,
    damping,
    stats,
    grad,
    out,
    sbuf,
    native,
    tiles,
    acc,
    partner_in,
    y_out,
    y_in,
    z_out,
    packed,
    off_r,
    off_s,
    r_mat,
    s_mat,
    inverse,
    g_rows,
    g_buf,
    q_buf,
    o_buf,
    o_all,
    stats_sem,
    local_sem,
    grad_send,
    grad_recv,
    part_send,
    part_recv,
    y_send,
    y_recv,
    z_send,
    x_send,
    x_recv,
    m_send,
    g_send,
    g_recv,
    out_send,
    out_recv,
    go,
):
    dp = lax.axis_index("dp")
    o = lax.axis_index("owner")
    h, c = dp // 2, dp % 2
    x, l, z = o % 4, (o // 4) % 2, o // 8
    quarter = W // 4
    half = W // 2

    def ring(t):
        return o - x + (x + t) % 4

    def y_place(step):
        y = (h * 2 + l + step) % 4
        return (y // 2) * 2 + c, z * 8 + (y % 2) * 4 + x

    def z_place(step):
        return dp, (o + 8 * step) % 32

    partner = (h * 2 + 1 - c, o)
    across = ((1 - h) * 2 + c, o)

    steps = sbuf.shape[1] // TOKEN_CHUNK

    def load(f, k):
        rows = pl.ds(k * TOKEN_CHUNK, TOKEN_CHUNK)
        return pltpu.make_async_copy(
            stats.at[f, rows], sbuf.at[f, rows], stats_sem.at[f * steps + k]
        )

    tiles_load = pltpu.make_async_copy(grad, native, local_sem.at[2])
    tiles_load.start()
    for f in range(2):
        for k in range(steps):
            load(f, k).start()
    mine = pl.ds(pl.multiple_of(dp * quarter, quarter), quarter)

    def own_tile(tau):
        return pltpu.make_async_copy(
            tiles.at[2 * c + tau], g_buf.at[tau, mine], local_sem.at[tau]
        )

    barrier = pltpu.get_barrier_semaphore()

    def greet(device):
        pl.semaphore_signal(barrier, inc=1, device_id=device, device_id_type=MESH)

    greet(partner)
    greet(across)
    greet(((1 - h) * 2 + 1 - c, o))

    @pl.when(c == 0)
    def _():
        greet((dp, ring(1)))
        greet((dp, ring(3)))
        greet((dp + 1, ring(2)))
        greet((dp + 1, ring(3)))
        for step in (1, 3):
            greet(y_place(step))
            greet(z_place(step))

    @pl.when(c == 1)
    def _():
        greet((dp - 1, ring(2)))
        greet((dp - 1, ring(1)))

    tiles_load.wait()
    tiles[...] = jnp.swapaxes(native[...], 0, 1)

    @pl.when(c == 0)
    def _():
        pl.semaphore_wait(barrier, 11)

    @pl.when(c == 1)
    def _():
        pl.semaphore_wait(barrier, 5)

    def grad_copy(rel, tau):
        to_h = h if rel < 2 else 1 - h
        to_c = c if rel % 2 == 0 else 1 - c
        n = (rel - 1) * 2 + tau
        return pltpu.make_async_remote_copy(
            src_ref=tiles.at[2 * to_c + tau],
            dst_ref=g_buf.at[tau, mine],
            send_sem=grad_send.at[n],
            recv_sem=grad_recv.at[n],
            device_id=(to_h * 2 + to_c, o),
            device_id_type=MESH,
        )

    def send_later_grads():
        grad_copy(3, 0).start()
        grad_copy(2, 1).start()
        grad_copy(3, 1).start()

    grad_copy(2, 0).start()
    for tau in range(2):
        own_tile(tau).start()

    def part_copy(k):
        rows = pl.ds(0, UPPER) if k == 0 else pl.ds(UPPER, TAIL - UPPER)
        return pltpu.make_async_remote_copy(
            src_ref=acc.at[1 - c, rows],
            dst_ref=partner_in.at[rows],
            send_sem=part_send.at[k],
            recv_sem=part_recv.at[k],
            device_id=partner,
            device_id_type=MESH,
        )

    def partial(f, _):
        for k in range(steps):
            load(f, k).wait()
            rows = slice(k * TOKEN_CHUNK, (k + 1) * TOKEN_CHUNK)
            for i in range(3):
                r = gram(sbuf[f, rows, i * N : (i + 1) * N], sbuf[f, rows, i * N :])
                for j in range(i, 3):
                    add_block(acc, f, i, j, r[:, (j - i) * N : (j - i + 1) * N], k == 0)

        @pl.when(f == 1 - c)
        def _():
            for k in range(2):
                part_copy(k).start()

        return 0

    lax.fori_loop(0, 2, partial, 0)
    grad_copy(1, 0).start()
    grad_copy(1, 1).start()
    bias = damping[c] * (0.5 * tokens)

    def sum_of_chip(k, diags):
        if k % 3 == 0:
            part_copy(k // 3).wait_recv()
        start, size = DATA[k]
        rows = slice(start, start + size)
        v = acc[c, rows, :] + partner_in[rows, :]
        acc[c, rows, :] = v
        y_out[rows, :] = v.astype(BF16)
        diags.extend(diagonals(k, v, bias))
        if k == 5:
            y_out[TAIL:ROWS, :] = pack_diagonal(diags)

    def y_copy(src, slot, device, k, send):
        start, size = CHUNKS[k]
        return pltpu.make_async_remote_copy(
            src_ref=src.at[pl.ds(start, size)],
            dst_ref=y_in.at[slot, pl.ds(start, size)],
            send_sem=y_send.at[send],
            recv_sem=y_recv.at[slot * 6 + k],
            device_id=device,
            device_id_type=MESH,
        )

    def y_plus(k):
        return y_copy(y_out, 0, y_place(1), k, k)

    def y_minus(k):
        return y_copy(y_out, 1, y_place(3), k, 6 + k)

    def y_on(k):
        if k < 3:
            return y_copy(y_in.at[0], 2, y_place(1), k, 12 + k)
        return y_copy(y_in.at[1], 2, y_place(3), k, 12 + k)

    def y_across(k):
        return y_copy(y_out, 2, across, k, k)

    def x_copy(t, k, slot):
        start, size = CHUNKS[k]
        to_slot = (1, 1, 2)[t - 1]
        return pltpu.make_async_remote_copy(
            src_ref=packed.at[slot, pl.ds(start, size)],
            dst_ref=packed.at[to_slot, pl.ds(start, size)],
            send_sem=x_send.at[(t - 1) * 6 + k],
            recv_sem=x_recv.at[to_slot * 6 + k],
            device_id=(dp + (0 if t == 1 else 1), ring(t)),
            device_id_type=MESH,
        )

    def z_copy(k):
        start, size = CHUNKS[k]
        return pltpu.make_async_remote_copy(
            src_ref=z_out.at[pl.ds(start, size)],
            dst_ref=packed.at[3, pl.ds(start, size)],
            send_sem=z_send.at[k],
            recv_sem=x_recv.at[18 + k],
            device_id=z_place(1),
            device_id_type=MESH,
        )

    def m_copy(k):
        start, size = CHUNKS[k]
        return pltpu.make_async_remote_copy(
            src_ref=packed.at[0, pl.ds(start, size)],
            dst_ref=packed.at[2, pl.ds(start, size)],
            send_sem=m_send.at[k],
            recv_sem=x_recv.at[12 + k],
            device_id=partner,
            device_id_type=MESH,
        )

    def sum_of_row(k, diags):
        start, size = DATA[k]
        rows = slice(start, start + size)
        packed[0, rows, :] = (acc[c, rows, :] + y_in[2, rows, :].astype(F32)).astype(BF16)
        if k == 5:
            other = unpack_diagonal(y_in[2, TAIL:ROWS, :])
            packed[0, TAIL:ROWS, :] = pack_diagonal([d + e for d, e in zip(diags, other)])

    def sum_of_other_row(k, dst):
        start, size = DATA[k]
        rows = slice(start, start + size)
        dst[rows, :] = (y_in[0, rows, :].astype(F32) + y_in[1, rows, :].astype(F32)).astype(BF16)
        if k == 5:
            one = unpack_diagonal(y_in[0, TAIL:ROWS, :])
            two = unpack_diagonal(y_in[1, TAIL:ROWS, :])
            dst[TAIL:ROWS, :] = pack_diagonal([d + e for d, e in zip(one, two)])

    def send_on(k, slot, ts):
        for t in ts:

            @pl.when((x + t < 4) if slot == 0 else (x + t >= 4))
            def _():
                x_copy(t, k, slot).start()

    @pl.when(c == 0)
    def _():
        diags = []
        for k in range(6):
            sum_of_chip(k, diags)
            if k < 3:
                y_plus(k).start()
            if k < 4:
                y_minus(k).start()

        def other_row(k):
            @pl.when(l == 0)
            def _():
                sum_of_other_row(k, z_out)
                z_copy(k).start()

            @pl.when(l == 1)
            def _():
                sum_of_other_row(k, packed.at[3])
                send_on(k, 3, (1, 2, 3))

        def from_z(k):
            @pl.when(l == 0)
            def _():
                z_copy(k).wait_recv()
                send_on(k, 3, (1, 2, 3))

        def own_row(k):
            y_on(k).wait_recv()
            sum_of_row(k, diags)
            send_on(k, 0, (1, 2, 3))

        for k in range(3):
            y_plus(k).wait_recv()
            y_on(k).start()
            y_plus(k + 3).start()
            y_minus(k).wait_recv()
            other_row(k)
            if k >= 2:
                from_z(k - 2)
        for k in range(3, 6):
            y_minus(k).wait_recv()
            y_on(k).start()
            if k < 5:
                y_minus(k + 1).start()
            else:
                pl.semaphore_signal(go, inc=1, device_id=partner, device_id_type=MESH)
            y_plus(k).wait_recv()
            other_row(k)
            from_z(k - 2)
            if k == 4:
                own_row(0)
        own_row(3)
        own_row(1)
        from_z(4)
        own_row(4)
        own_row(2)
        from_z(5)
        own_row(5)
        send_later_grads()
    @pl.when(c == 1)
    def _():
        diags = []
        for k in range(6):
            sum_of_chip(k, diags)
        pl.semaphore_wait(go, 1)
        for k in range(6):
            y_across(k).start()
        for k in range(6):
            y_across(k).wait_recv()
            sum_of_row(k, diags)
            m_copy(k).start()
        send_later_grads()

    g_copy = pltpu.make_async_remote_copy(
        src_ref=g_rows,
        dst_ref=g_rows,
        send_sem=g_send.at[0],
        recv_sem=g_recv.at[0],
        device_id=partner,
        device_id_type=MESH,
    )
    chip_rows = pl.ds(pl.multiple_of(h * half, half), half)

    def one(n, _):
        slot = (1 - c) * ((2 * n) % 3) + c * ((n + 1) % 3)

        @pl.when((c == 0) | (n < 2))
        def _():
            @pl.when(slot >= 1)
            def _():
                for k in range(6):
                    start, size = CHUNKS[k]
                    pltpu.make_async_remote_copy(
                        src_ref=packed.at[0, pl.ds(start, size)],
                        dst_ref=packed.at[1, pl.ds(start, size)],
                        send_sem=m_send.at[k],
                        recv_sem=x_recv.at[slot * 6 + k],
                        device_id=partner,
                        device_id_type=MESH,
                    ).wait_recv()

            invert(packed.at[slot], tokens, off_r, off_s, r_mat, s_mat, inverse.at[slot])

            @pl.when((c == 0) & (n == 1))
            def _():
                g_rows[...] = inverse[2, chip_rows, :]
                g_copy.start()

        return 0

    lax.fori_loop(0, 3, one, 0)

    @pl.when(c == 1)
    def _():
        g_copy.wait_recv()

    own_rows = pl.ds(pl.multiple_of(c * quarter, quarter), quarter)
    other_rows = pl.ds(pl.multiple_of((1 - c) * quarter, quarter), quarter)

    def out_copy(tau):
        return pltpu.make_async_remote_copy(
            src_ref=o_buf.at[tau],
            dst_ref=o_all.at[2 * c + tau],
            send_sem=out_send.at[tau],
            recv_sem=out_recv.at[tau],
            device_id=partner,
            device_id_type=MESH,
        )

    def tile(tau, _):
        own_tile(tau).wait()
        for rel in (1, 2, 3):
            grad_copy(rel, tau).wait_recv()
        q_buf[...] = jnp.dot(g_rows[...], g_buf[tau], preferred_element_type=F32).astype(BF16)
        a = inverse.at[tau + c]
        o_buf[tau] = jnp.dot(q_buf[other_rows, :], a[...], preferred_element_type=F32).astype(BF16)
        out_copy(tau).start()
        o_all[2 * c + tau] = jnp.dot(q_buf[own_rows, :], a[...], preferred_element_type=F32).astype(
            BF16
        )
        return 0

    lax.fori_loop(0, 2, tile, 0)

    for k in range(2):
        part_copy(k).wait_send()
    for rel in (1, 2, 3):
        for tau in range(2):
            grad_copy(rel, tau).wait_send()

    @pl.when(c == 1)
    def _():
        for k in range(6):
            y_across(k).wait_send()
            m_copy(k).wait_send()

    @pl.when(c == 0)
    def _():
        g_copy.wait_send()
        for k in range(6):
            y_plus(k).wait_send()
            y_minus(k).wait_send()
            y_on(k).wait_send()

            @pl.when(l == 0)
            def _():
                z_copy(k).wait_send()

            for t in range(1, 4):
                x_copy(t, k, 0).wait_send()

    for tau in range(2):
        out_copy(tau).wait()
    out[...] = jnp.swapaxes(o_all[...], 0, 1)


def per_device(stats, damping, grad, total_tokens):
    local_tokens = stats.shape[2]
    quarter, band, width = grad.shape[1:]
    dma = pltpu.SemaphoreType.DMA
    result = pl.pallas_call(
        functools.partial(kernel, float(total_tokens)),
        out_shape=jax.ShapeDtypeStruct((quarter, band, width), BF16),
        in_specs=[
            pl.BlockSpec(memory_space=pltpu.SMEM),
            pl.BlockSpec(memory_space=pl.ANY),
            pl.BlockSpec(memory_space=pl.ANY),
        ],
        out_specs=pl.BlockSpec(memory_space=pltpu.VMEM),
        scratch_shapes=[
            pltpu.VMEM((2, local_tokens, width), BF16),
            pltpu.VMEM((quarter, band, width), BF16),
            pltpu.VMEM((band, quarter, width), BF16),
            pltpu.VMEM((2, TAIL, N), F32),
            pltpu.VMEM((TAIL, N), F32),
            pltpu.VMEM((ROWS, N), BF16),
            pltpu.VMEM((3, ROWS, N), BF16),
            pltpu.VMEM((ROWS, N), BF16),
            pltpu.VMEM((4, ROWS, N), BF16),
            pltpu.VMEM((6, N, N), F32),
            pltpu.VMEM((6, N, N), F32),
            pltpu.VMEM((3, W, W), BF16),
            pltpu.VMEM((2, W, W), BF16),
            pltpu.VMEM((3, W, W), BF16),
            pltpu.VMEM((W // 2, W), BF16),
            pltpu.VMEM((2, W, W), BF16),
            pltpu.VMEM((W // 2, W), BF16),
            pltpu.VMEM((2, W // 4, W), BF16),
            pltpu.VMEM((band, quarter, width), BF16),
            dma((2 * local_tokens // TOKEN_CHUNK,)),
            dma((3,)),
            dma((6,)),
            dma((6,)),
            dma((2,)),
            dma((2,)),
            dma((18,)),
            dma((18,)),
            dma((6,)),
            dma((18,)),
            dma((24,)),
            dma((6,)),
            dma((1,)),
            dma((1,)),
            dma((2,)),
            dma((2,)),
            pltpu.SemaphoreType.REGULAR,
        ],
        compiler_params=pltpu.CompilerParams(
            collective_id=0, has_side_effects=True, vmem_limit_bytes=56 * 2**20
        ),
    )(damping[0], stats[0], grad[0])
    return result[None]


def solution(mesh):
    in_specs = (P("owner", None, "dp", None), P("owner", None), P("owner", "dp", None, None))
    out_specs = P("owner", "dp", None, None)

    def whole(stats, damping, grad):
        def one(s, d, g):
            return per_device(s, d, g, stats.shape[2])

        return jax.shard_map(
            one, mesh=mesh, in_specs=in_specs, out_specs=out_specs, check_vma=False
        )(stats, damping, grad)

    return whole
```

```python
import functools

import jax
import jax.numpy as jnp
from jax import lax
from jax.experimental import pallas as pl
from jax.experimental.pallas import tpu as pltpu
from jax.sharding import PartitionSpec as P

MESH = pl.DeviceIdType.MESH
F32 = jnp.float32
BF16 = jnp.bfloat16
N = 256
W = 768
PAIRS = ((0, 0), (0, 1), (0, 2), (1, 1), (1, 2), (2, 2))
H = N // 2
OFF = {(0, 1): 0, (0, 2): N, (1, 2): 2 * N}
UPPER = 3 * N
LOWER = UPPER + 3 * H
TAIL = LOWER + H + H // 2
ROWS = TAIL + 16
CHUNKS = tuple((k * N, N if k < 5 else ROWS - 5 * N) for k in range(6))
DATA = tuple((k * N, N if k < 5 else TAIL - 5 * N) for k in range(6))
TOKEN_CHUNK = 1024


def eye_mask():
    shape = (N, N)
    return lax.broadcasted_iota(jnp.int32, shape, 0) == lax.broadcasted_iota(jnp.int32, shape, 1)


def gram(a, b):
    return lax.dot_general(a, b, (((0,), (0,)), ((), ())), preferred_element_type=F32)


def pack_diagonal(diags):
    row = lax.broadcasted_iota(jnp.int32, (16, N), 0)
    out = jnp.zeros((16, N), F32)
    for i, d in enumerate(diags):
        high = d.astype(BF16).astype(F32)
        out = jnp.where(row == i, high, out)
        out = jnp.where(row == i + 5, d - high, out)
    return out.astype(BF16)


def unpack_diagonal(tail):
    t = tail.astype(F32)
    return [t[i : i + 1] + t[i + 5 : i + 6] for i in range(5)]


def add_block(acc, f, i, j, v, first):
    def put(rows, columns, w):
        if first:
            acc[f, rows, columns] = w
        else:
            acc[f, rows, columns] += w

    full = slice(0, N)
    if i != j:
        put(slice(OFF[i, j], OFF[i, j] + N), full, v)
        return
    put(slice(UPPER + i * H, UPPER + (i + 1) * H), full, v[:H])
    low = v[H:, H:]
    if i < 2:
        put(slice(LOWER, LOWER + H), slice(i * H, (i + 1) * H), low)
    else:
        rows = slice(LOWER + H, TAIL)
        put(rows, slice(0, H), low[: H // 2])
        put(rows, slice(H, N), low[H // 2 :])


def diagonals(k, v, bias):
    def pick(w, mask):
        return jnp.sum(jnp.where(mask, w + bias, 0.0), axis=0, keepdims=True)

    row = lax.broadcasted_iota(jnp.int32, (H, N), 0)
    lane = lax.broadcasted_iota(jnp.int32, (H, N), 1)
    if k == 3:
        return [pick(v[:H], row == lane), pick(v[H:], row == lane)]
    if k == 4:
        return [pick(v[:H], row == lane), pick(v[H:], row == lane % H)]
    if k == 5:
        row, lane = row[: H // 2], lane[: H // 2]
        return [pick(v, (lane == row) | (lane == row + H + H // 2))]
    return []


def invert(packed, tokens, off_r, off_s, r_mat, s_mat, result):
    eye = eye_mask()
    parts = [d * (1.0 / tokens) for d in unpack_diagonal(packed[TAIL:ROWS, :])]
    seconds = [parts[3][:, :H], parts[3][:, H:], parts[4][:, :H] + parts[4][:, H:]]
    diag = [jnp.concatenate([parts[i][:, :H], seconds[i]], axis=1) for i in range(3)]
    sums = [None] * 3

    def add(i, v):
        sums[i] = v if sums[i] is None else sums[i] + v

    def unpack(i, j):
        if i != j:
            return packed[OFF[i, j] : OFF[i, j] + N, :].astype(F32)
        top = packed[UPPER + i * H : UPPER + (i + 1) * H, :].astype(F32)
        if i < 2:
            low = packed[LOWER : LOWER + H, i * H : (i + 1) * H].astype(F32)
        else:
            both = packed[LOWER + H : TAIL, :].astype(F32)
            low = jnp.concatenate([both[:, :H], both[:, H:]], axis=0)
        bottom = jnp.concatenate([top[:, H:].T, low], axis=1)
        return jnp.concatenate([top, bottom], axis=0)

    for b, (i, j) in enumerate(PAIRS):
        v = unpack(i, j) * (1.0 / tokens)
        if i == j:
            v = jnp.where(eye, 0.0, v)
        off_r[b] = v
        a = jnp.abs(v)
        add(j, jnp.sum(a, axis=0, keepdims=True))
        if i != j:
            add(i, jnp.sum(a.T, axis=0, keepdims=True))
    sums = [s + jnp.abs(d) for s, d in zip(sums, diag)]
    factor = 1.0 / jnp.max(jnp.maximum(jnp.maximum(sums[0], sums[1]), sums[2]))
    d_row = [1.0 - factor * d for d in diag]
    d_col = [
        jnp.sum(jnp.where(eye, jnp.broadcast_to(d, (N, N)), 0.0), axis=1, keepdims=True)
        for d in d_row
    ]

    def put(ref, i, j, v):
        ref[i * N : (i + 1) * N, j * N : (j + 1) * N] = v.astype(BF16)
        if i != j:
            ref[j * N : (j + 1) * N, i * N : (i + 1) * N] = v.T.astype(BF16)

    for b, (i, j) in enumerate(PAIRS):
        v = off_r[b] * (-factor)
        off_r[b] = v
        off_s[b] = v
        put(r_mat.at[0], i, j, v)
    s_row = [1.0 + d for d in d_row]
    s_col = [1.0 + d for d in d_col]

    def product(a, b, i, j):
        return jnp.dot(
            a[i * N : (i + 1) * N, :], b[:, j * N : (j + 1) * N], preferred_element_type=F32
        )

    def square(src, dst):
        for b, (i, j) in enumerate(PAIRS):
            v = off_r[b] * (d_col[i] + d_row[j]) + product(src, src, i, j)
            off_r[b] = v
            put(dst, i, j, v)

    square(r_mat.at[0], r_mat.at[1])
    d_row = [d * d for d in d_row]
    d_col = [d * d for d in d_col]
    now = 1
    left = r_mat.at[0]
    for k in range(4):
        last = k == 3
        for b, (i, j) in enumerate(PAIRS):
            v = s_col[i] * off_r[b] + off_s[b] * (1.0 + d_row[j])
            v = v + product(left, r_mat.at[now], i, j)
            if last:
                if i == j:
                    v = v + jnp.where(eye, s_row[j] * (1.0 + d_row[j]), 0.0)
                put(result, i, j, v * factor)
            else:
                off_s[b] = v
                put(s_mat.at[k % 2], i, j, v)
        if not last:
            s_row = [s * (1.0 + d) for s, d in zip(s_row, d_row)]
            s_col = [s * (1.0 + d) for s, d in zip(s_col, d_col)]
            left = s_mat.at[k % 2]
            square(r_mat.at[now], r_mat.at[3 - now])
            now = 3 - now
            d_row = [d * d for d in d_row]
            d_col = [d * d for d in d_col]


def kernel(
    tokens,
    damping,
    stats,
    grad,
    o_all,
    sbuf,
    native,
    tiles,
    acc,
    partner_in,
    y_out,
    y_in,
    z_out,
    packed,
    off_r,
    off_s,
    r_mat,
    s_mat,
    inverse,
    g_rows,
    g_buf,
    q_buf,
    o_buf,
    stats_sem,
    local_sem,
    grad_send,
    grad_recv,
    part_send,
    part_recv,
    y_send,
    y_recv,
    z_send,
    x_send,
    x_recv,
    m_send,
    g_send,
    g_recv,
    out_send,
    out_recv,
    go,
):
    dp = lax.axis_index("dp")
    o = lax.axis_index("owner")
    h, c = dp // 2, dp % 2
    x, l, z = o % 4, (o // 4) % 2, o // 8
    quarter = W // 4
    half = W // 2

    def ring(t):
        return o - x + (x + t) % 4

    def y_place(step):
        y = (h * 2 + l + step) % 4
        return (y // 2) * 2 + c, z * 8 + (y % 2) * 4 + x

    def z_place(step):
        return dp, (o + 8 * step) % 32

    partner = (h * 2 + 1 - c, o)
    across = ((1 - h) * 2 + c, o)

    steps = sbuf.shape[1] // TOKEN_CHUNK

    def load(f, k):
        rows = pl.ds(k * TOKEN_CHUNK, TOKEN_CHUNK)
        return pltpu.make_async_copy(
            stats.at[f, rows], sbuf.at[f, rows], stats_sem.at[f * steps + k]
        )

    tiles_load = pltpu.make_async_copy(grad, native, local_sem.at[2])
    tiles_load.start()
    for f in range(2):
        for k in range(steps):
            load(f, k).start()
    mine = pl.ds(pl.multiple_of(dp * quarter, quarter), quarter)

    def own_tile(tau):
        return pltpu.make_async_copy(
            tiles.at[2 * c + tau], g_buf.at[tau, mine], local_sem.at[tau]
        )

    barrier = pltpu.get_barrier_semaphore()

    def greet(device):
        pl.semaphore_signal(barrier, inc=1, device_id=device, device_id_type=MESH)

    greet(partner)
    greet(across)
    greet(((1 - h) * 2 + 1 - c, o))

    @pl.when(c == 0)
    def _():
        greet((dp, ring(1)))
        greet((dp, ring(3)))
        greet((dp + 1, ring(2)))
        greet((dp + 1, ring(3)))
        for step in (1, 3):
            greet(y_place(step))
            greet(z_place(step))

    @pl.when(c == 1)
    def _():
        greet((dp - 1, ring(2)))
        greet((dp - 1, ring(1)))

    tiles_load.wait()
    tiles[...] = jnp.swapaxes(native[...], 0, 1)

    @pl.when(c == 0)
    def _():
        pl.semaphore_wait(barrier, 11)

    @pl.when(c == 1)
    def _():
        pl.semaphore_wait(barrier, 5)

    def grad_copy(rel, tau):
        to_h = h if rel < 2 else 1 - h
        to_c = c if rel % 2 == 0 else 1 - c
        n = (rel - 1) * 2 + tau
        return pltpu.make_async_remote_copy(
            src_ref=tiles.at[2 * to_c + tau],
            dst_ref=g_buf.at[tau, mine],
            send_sem=grad_send.at[n],
            recv_sem=grad_recv.at[n],
            device_id=(to_h * 2 + to_c, o),
            device_id_type=MESH,
        )

    def send_later_grads():
        grad_copy(3, 0).start()
        grad_copy(2, 1).start()
        grad_copy(3, 1).start()

    grad_copy(2, 0).start()
    for tau in range(2):
        own_tile(tau).start()

    def part_copy(k):
        rows = pl.ds(0, UPPER) if k == 0 else pl.ds(UPPER, TAIL - UPPER)
        return pltpu.make_async_remote_copy(
            src_ref=acc.at[1 - c, rows],
            dst_ref=partner_in.at[rows],
            send_sem=part_send.at[k],
            recv_sem=part_recv.at[k],
            device_id=partner,
            device_id_type=MESH,
        )

    def partial(f, _):
        for k in range(steps):
            load(f, k).wait()
            rows = slice(k * TOKEN_CHUNK, (k + 1) * TOKEN_CHUNK)
            for i in range(3):
                r = gram(sbuf[f, rows, i * N : (i + 1) * N], sbuf[f, rows, i * N :])
                for j in range(i, 3):
                    add_block(acc, f, i, j, r[:, (j - i) * N : (j - i + 1) * N], k == 0)

        @pl.when(f == 1 - c)
        def _():
            for k in range(2):
                part_copy(k).start()

        return 0

    lax.fori_loop(0, 2, partial, 0)
    grad_copy(1, 0).start()
    grad_copy(1, 1).start()
    bias = damping[c] * (0.5 * tokens)

    def sum_of_chip(k, diags):
        if k % 3 == 0:
            part_copy(k // 3).wait_recv()
        start, size = DATA[k]
        rows = slice(start, start + size)
        v = acc[c, rows, :] + partner_in[rows, :]
        acc[c, rows, :] = v
        y_out[rows, :] = v.astype(BF16)
        diags.extend(diagonals(k, v, bias))
        if k == 5:
            y_out[TAIL:ROWS, :] = pack_diagonal(diags)

    def y_copy(src, slot, device, k, send):
        start, size = CHUNKS[k]
        return pltpu.make_async_remote_copy(
            src_ref=src.at[pl.ds(start, size)],
            dst_ref=y_in.at[slot, pl.ds(start, size)],
            send_sem=y_send.at[send],
            recv_sem=y_recv.at[slot * 6 + k],
            device_id=device,
            device_id_type=MESH,
        )

    def y_plus(k):
        return y_copy(y_out, 0, y_place(1), k, k)

    def y_minus(k):
        return y_copy(y_out, 1, y_place(3), k, 6 + k)

    def y_on(k):
        if k < 3:
            return y_copy(y_in.at[0], 2, y_place(1), k, 12 + k)
        return y_copy(y_in.at[1], 2, y_place(3), k, 12 + k)

    def y_across(k):
        return y_copy(y_out, 2, across, k, k)

    def x_copy(t, k, slot):
        start, size = CHUNKS[k]
        to_slot = (1, 1, 2)[t - 1]
        return pltpu.make_async_remote_copy(
            src_ref=packed.at[slot, pl.ds(start, size)],
            dst_ref=packed.at[to_slot, pl.ds(start, size)],
            send_sem=x_send.at[(t - 1) * 6 + k],
            recv_sem=x_recv.at[to_slot * 6 + k],
            device_id=(dp + (0 if t == 1 else 1), ring(t)),
            device_id_type=MESH,
        )

    def z_copy(k):
        start, size = CHUNKS[k]
        return pltpu.make_async_remote_copy(
            src_ref=z_out.at[pl.ds(start, size)],
            dst_ref=packed.at[3, pl.ds(start, size)],
            send_sem=z_send.at[k],
            recv_sem=x_recv.at[18 + k],
            device_id=z_place(1),
            device_id_type=MESH,
        )

    def m_copy(k):
        start, size = CHUNKS[k]
        return pltpu.make_async_remote_copy(
            src_ref=packed.at[0, pl.ds(start, size)],
            dst_ref=packed.at[2, pl.ds(start, size)],
            send_sem=m_send.at[k],
            recv_sem=x_recv.at[12 + k],
            device_id=partner,
            device_id_type=MESH,
        )

    def sum_of_row(k, diags):
        start, size = DATA[k]
        rows = slice(start, start + size)
        packed[0, rows, :] = (acc[c, rows, :] + y_in[2, rows, :].astype(F32)).astype(BF16)
        if k == 5:
            other = unpack_diagonal(y_in[2, TAIL:ROWS, :])
            packed[0, TAIL:ROWS, :] = pack_diagonal([d + e for d, e in zip(diags, other)])

    def sum_of_other_row(k, dst):
        start, size = DATA[k]
        rows = slice(start, start + size)
        dst[rows, :] = (y_in[0, rows, :].astype(F32) + y_in[1, rows, :].astype(F32)).astype(BF16)
        if k == 5:
            one = unpack_diagonal(y_in[0, TAIL:ROWS, :])
            two = unpack_diagonal(y_in[1, TAIL:ROWS, :])
            dst[TAIL:ROWS, :] = pack_diagonal([d + e for d, e in zip(one, two)])

    def send_on(k, slot, ts):
        for t in ts:

            @pl.when((x + t < 4) if slot == 0 else (x + t >= 4))
            def _():
                x_copy(t, k, slot).start()

    @pl.when(c == 0)
    def _():
        diags = []
        for k in range(6):
            sum_of_chip(k, diags)
            if k < 3:
                y_plus(k).start()
            if k < 4:
                y_minus(k).start()

        def other_row(k):
            @pl.when(l == 0)
            def _():
                sum_of_other_row(k, z_out)
                z_copy(k).start()

            @pl.when(l == 1)
            def _():
                sum_of_other_row(k, packed.at[3])
                send_on(k, 3, (1, 2, 3))

        def from_z(k):
            @pl.when(l == 0)
            def _():
                z_copy(k).wait_recv()
                send_on(k, 3, (1, 2, 3))

        def own_row(k):
            y_on(k).wait_recv()
            sum_of_row(k, diags)
            send_on(k, 0, (1, 2, 3))

        for k in range(3):
            y_plus(k).wait_recv()
            y_on(k).start()
            y_plus(k + 3).start()
            y_minus(k).wait_recv()
            other_row(k)
            if k >= 2:
                from_z(k - 2)
        for k in range(3, 6):
            y_minus(k).wait_recv()
            y_on(k).start()
            if k < 5:
                y_minus(k + 1).start()
            if k == 4:
                pl.semaphore_signal(go, inc=1, device_id=partner, device_id_type=MESH)
            y_plus(k).wait_recv()
            other_row(k)
            from_z(k - 2)
            if k == 4:
                own_row(0)
        own_row(3)
        own_row(1)
        from_z(4)
        own_row(4)
        own_row(2)
        from_z(5)
        own_row(5)
        send_later_grads()
    @pl.when(c == 1)
    def _():
        diags = []
        for k in range(6):
            sum_of_chip(k, diags)
        pl.semaphore_wait(go, 1)
        for k in range(6):
            y_across(k).start()
        for k in range(6):
            y_across(k).wait_recv()
            sum_of_row(k, diags)
            m_copy(k).start()
        send_later_grads()

    g_copy = pltpu.make_async_remote_copy(
        src_ref=g_rows,
        dst_ref=g_rows,
        send_sem=g_send.at[0],
        recv_sem=g_recv.at[0],
        device_id=partner,
        device_id_type=MESH,
    )
    chip_rows = pl.ds(pl.multiple_of(h * half, half), half)

    def one(n, _):
        slot = (1 - c) * ((2 * n) % 3) + c * ((n + 1) % 3)

        @pl.when((c == 0) | (n < 2))
        def _():
            @pl.when(slot >= 1)
            def _():
                for k in range(6):
                    start, size = CHUNKS[k]
                    pltpu.make_async_remote_copy(
                        src_ref=packed.at[0, pl.ds(start, size)],
                        dst_ref=packed.at[1, pl.ds(start, size)],
                        send_sem=m_send.at[k],
                        recv_sem=x_recv.at[slot * 6 + k],
                        device_id=partner,
                        device_id_type=MESH,
                    ).wait_recv()

            invert(packed.at[slot], tokens, off_r, off_s, r_mat, s_mat, inverse.at[slot])

            @pl.when((c == 0) & (n == 1))
            def _():
                g_rows[...] = inverse[2, chip_rows, :]
                g_copy.start()

        return 0

    lax.fori_loop(0, 3, one, 0)

    @pl.when(c == 1)
    def _():
        g_copy.wait_recv()

    own_rows = pl.ds(pl.multiple_of(c * quarter, quarter), quarter)
    other_rows = pl.ds(pl.multiple_of((1 - c) * quarter, quarter), quarter)

    def out_copy(tau):
        return pltpu.make_async_remote_copy(
            src_ref=o_buf.at[tau],
            dst_ref=o_all.at[2 * c + tau],
            send_sem=out_send.at[tau],
            recv_sem=out_recv.at[tau],
            device_id=partner,
            device_id_type=MESH,
        )

    def tile(tau, _):
        own_tile(tau).wait()
        for rel in (1, 2, 3):
            grad_copy(rel, tau).wait_recv()
        q_buf[...] = jnp.dot(g_rows[...], g_buf[tau], preferred_element_type=F32).astype(BF16)
        a = inverse.at[tau + c]
        o_buf[tau] = jnp.dot(q_buf[other_rows, :], a[...], preferred_element_type=F32).astype(BF16)
        out_copy(tau).start()
        o_all[2 * c + tau] = jnp.dot(q_buf[own_rows, :], a[...], preferred_element_type=F32).astype(
            BF16
        )
        return 0

    lax.fori_loop(0, 2, tile, 0)

    for k in range(2):
        part_copy(k).wait_send()
    for rel in (1, 2, 3):
        for tau in range(2):
            grad_copy(rel, tau).wait_send()

    @pl.when(c == 1)
    def _():
        for k in range(6):
            y_across(k).wait_send()
            m_copy(k).wait_send()

    @pl.when(c == 0)
    def _():
        g_copy.wait_send()
        for k in range(6):
            y_plus(k).wait_send()
            y_minus(k).wait_send()
            y_on(k).wait_send()

            @pl.when(l == 0)
            def _():
                z_copy(k).wait_send()

            for t in range(1, 4):
                x_copy(t, k, 0).wait_send()

    for tau in range(2):
        out_copy(tau).wait()


def rows_first(by_tile, out):
    out[...] = jnp.swapaxes(by_tile[...], 0, 1)


def per_device(stats, damping, grad, total_tokens):
    local_tokens = stats.shape[2]
    quarter, band, width = grad.shape[1:]
    dma = pltpu.SemaphoreType.DMA
    result = pl.pallas_call(
        functools.partial(kernel, float(total_tokens)),
        out_shape=jax.ShapeDtypeStruct((band, quarter, width), BF16),
        in_specs=[
            pl.BlockSpec(memory_space=pltpu.SMEM),
            pl.BlockSpec(memory_space=pl.ANY),
            pl.BlockSpec(memory_space=pl.ANY),
        ],
        out_specs=pl.BlockSpec(memory_space=pltpu.VMEM),
        scratch_shapes=[
            pltpu.VMEM((2, local_tokens, width), BF16),
            pltpu.VMEM((quarter, band, width), BF16),
            pltpu.VMEM((band, quarter, width), BF16),
            pltpu.VMEM((2, TAIL, N), F32),
            pltpu.VMEM((TAIL, N), F32),
            pltpu.VMEM((ROWS, N), BF16),
            pltpu.VMEM((3, ROWS, N), BF16),
            pltpu.VMEM((ROWS, N), BF16),
            pltpu.VMEM((4, ROWS, N), BF16),
            pltpu.VMEM((6, N, N), F32),
            pltpu.VMEM((6, N, N), F32),
            pltpu.VMEM((3, W, W), BF16),
            pltpu.VMEM((2, W, W), BF16),
            pltpu.VMEM((3, W, W), BF16),
            pltpu.VMEM((W // 2, W), BF16),
            pltpu.VMEM((2, W, W), BF16),
            pltpu.VMEM((W // 2, W), BF16),
            pltpu.VMEM((2, W // 4, W), BF16),
            dma((2 * local_tokens // TOKEN_CHUNK,)),
            dma((3,)),
            dma((6,)),
            dma((6,)),
            dma((2,)),
            dma((2,)),
            dma((18,)),
            dma((18,)),
            dma((6,)),
            dma((18,)),
            dma((24,)),
            dma((6,)),
            dma((1,)),
            dma((1,)),
            dma((2,)),
            dma((2,)),
            pltpu.SemaphoreType.REGULAR,
        ],
        compiler_params=pltpu.CompilerParams(
            collective_id=0, has_side_effects=True, vmem_limit_bytes=56 * 2**20
        ),
    )(damping[0], stats[0], grad[0])
    return pl.pallas_call(
        rows_first,
        out_shape=jax.ShapeDtypeStruct((quarter, band, width), BF16),
        in_specs=[pl.BlockSpec(memory_space=pltpu.VMEM)],
        out_specs=pl.BlockSpec(memory_space=pltpu.VMEM),
    )(result)[None]


def solution(mesh):
    in_specs = (P("owner", None, "dp", None), P("owner", None), P("owner", "dp", None, None))
    out_specs = P("owner", "dp", None, None)

    def whole(stats, damping, grad):
        def one(s, d, g):
            return per_device(s, d, g, stats.shape[2])

        return jax.shard_map(
            one, mesh=mesh, in_specs=in_specs, out_specs=out_specs, check_vma=False
        )(stats, damping, grad)

    return whole
```

```python
import functools

import jax
import jax.numpy as jnp
from jax import lax
from jax.experimental import pallas as pl
from jax.experimental.pallas import tpu as pltpu
from jax.sharding import PartitionSpec as P

MESH = pl.DeviceIdType.MESH
F32 = jnp.float32
BF16 = jnp.bfloat16
N = 256
W = 768
PAIRS = ((0, 0), (0, 1), (0, 2), (1, 1), (1, 2), (2, 2))
H = N // 2
OFF = {(0, 1): 0, (0, 2): N, (1, 2): 2 * N}
UPPER = 3 * N
LOWER = UPPER + 3 * H
TAIL = LOWER + H + H // 2
ROWS = TAIL + 16
CHUNKS = tuple((k * N, N if k < 5 else ROWS - 5 * N) for k in range(6))
DATA = tuple((k * N, N if k < 5 else TAIL - 5 * N) for k in range(6))
TOKEN_CHUNK = 1024


def eye_mask():
    shape = (N, N)
    return lax.broadcasted_iota(jnp.int32, shape, 0) == lax.broadcasted_iota(jnp.int32, shape, 1)


def gram(a, b):
    return lax.dot_general(a, b, (((0,), (0,)), ((), ())), preferred_element_type=F32)


def pack_diagonal(diags):
    row = lax.broadcasted_iota(jnp.int32, (16, N), 0)
    out = jnp.zeros((16, N), F32)
    for i, d in enumerate(diags):
        high = d.astype(BF16).astype(F32)
        out = jnp.where(row == i, high, out)
        out = jnp.where(row == i + 5, d - high, out)
    return out.astype(BF16)


def unpack_diagonal(tail):
    t = tail.astype(F32)
    return [t[i : i + 1] + t[i + 5 : i + 6] for i in range(5)]


def add_block(acc, f, i, j, v, first):
    def put(rows, columns, w):
        if first:
            acc[f, rows, columns] = w
        else:
            acc[f, rows, columns] += w

    full = slice(0, N)
    if i != j:
        put(slice(OFF[i, j], OFF[i, j] + N), full, v)
        return
    put(slice(UPPER + i * H, UPPER + (i + 1) * H), full, v[:H])
    low = v[H:, H:]
    if i < 2:
        put(slice(LOWER, LOWER + H), slice(i * H, (i + 1) * H), low)
    else:
        rows = slice(LOWER + H, TAIL)
        put(rows, slice(0, H), low[: H // 2])
        put(rows, slice(H, N), low[H // 2 :])


def diagonals(k, v, bias):
    def pick(w, mask):
        return jnp.sum(jnp.where(mask, w + bias, 0.0), axis=0, keepdims=True)

    row = lax.broadcasted_iota(jnp.int32, (H, N), 0)
    lane = lax.broadcasted_iota(jnp.int32, (H, N), 1)
    if k == 3:
        return [pick(v[:H], row == lane), pick(v[H:], row == lane)]
    if k == 4:
        return [pick(v[:H], row == lane), pick(v[H:], row == lane % H)]
    if k == 5:
        row, lane = row[: H // 2], lane[: H // 2]
        return [pick(v, (lane == row) | (lane == row + H + H // 2))]
    return []


def invert(packed, tokens, off_r, off_s, r_mat, s_mat, result):
    eye = eye_mask()
    parts = [d * (1.0 / tokens) for d in unpack_diagonal(packed[TAIL:ROWS, :])]
    seconds = [parts[3][:, :H], parts[3][:, H:], parts[4][:, :H] + parts[4][:, H:]]
    diag = [jnp.concatenate([parts[i][:, :H], seconds[i]], axis=1) for i in range(3)]
    sums = [None] * 3

    def add(i, v):
        sums[i] = v if sums[i] is None else sums[i] + v

    def unpack(i, j):
        if i != j:
            return packed[OFF[i, j] : OFF[i, j] + N, :].astype(F32)
        top = packed[UPPER + i * H : UPPER + (i + 1) * H, :].astype(F32)
        if i < 2:
            low = packed[LOWER : LOWER + H, i * H : (i + 1) * H].astype(F32)
        else:
            both = packed[LOWER + H : TAIL, :].astype(F32)
            low = jnp.concatenate([both[:, :H], both[:, H:]], axis=0)
        bottom = jnp.concatenate([top[:, H:].T, low], axis=1)
        return jnp.concatenate([top, bottom], axis=0)

    for b, (i, j) in enumerate(PAIRS):
        v = unpack(i, j) * (1.0 / tokens)
        if i == j:
            v = jnp.where(eye, 0.0, v)
        off_r[b] = v
        a = jnp.abs(v)
        add(j, jnp.sum(a, axis=0, keepdims=True))
        if i != j:
            add(i, jnp.sum(a.T, axis=0, keepdims=True))
    sums = [s + jnp.abs(d) for s, d in zip(sums, diag)]
    factor = 1.0 / jnp.max(jnp.maximum(jnp.maximum(sums[0], sums[1]), sums[2]))
    d_row = [1.0 - factor * d for d in diag]
    d_col = [
        jnp.sum(jnp.where(eye, jnp.broadcast_to(d, (N, N)), 0.0), axis=1, keepdims=True)
        for d in d_row
    ]

    def put(ref, i, j, v):
        ref[i * N : (i + 1) * N, j * N : (j + 1) * N] = v.astype(BF16)
        if i != j:
            ref[j * N : (j + 1) * N, i * N : (i + 1) * N] = v.T.astype(BF16)

    for b, (i, j) in enumerate(PAIRS):
        v = off_r[b] * (-factor)
        off_r[b] = v
        off_s[b] = v
        put(r_mat.at[0], i, j, v)
    s_row = [1.0 + d for d in d_row]
    s_col = [1.0 + d for d in d_col]

    def product(a, b, i, j):
        return jnp.dot(
            a[i * N : (i + 1) * N, :], b[:, j * N : (j + 1) * N], preferred_element_type=F32
        )

    def square(src, dst):
        for b, (i, j) in enumerate(PAIRS):
            v = off_r[b] * (d_col[i] + d_row[j]) + product(src, src, i, j)
            off_r[b] = v
            put(dst, i, j, v)

    square(r_mat.at[0], r_mat.at[1])
    d_row = [d * d for d in d_row]
    d_col = [d * d for d in d_col]
    now = 1
    left = r_mat.at[0]
    for k in range(4):
        last = k == 3
        for b, (i, j) in enumerate(PAIRS):
            v = s_col[i] * off_r[b] + off_s[b] * (1.0 + d_row[j])
            v = v + product(left, r_mat.at[now], i, j)
            if last:
                if i == j:
                    v = v + jnp.where(eye, s_row[j] * (1.0 + d_row[j]), 0.0)
                put(result, i, j, v * factor)
            else:
                off_s[b] = v
                put(s_mat.at[k % 2], i, j, v)
        if not last:
            s_row = [s * (1.0 + d) for s, d in zip(s_row, d_row)]
            s_col = [s * (1.0 + d) for s, d in zip(s_col, d_col)]
            left = s_mat.at[k % 2]
            square(r_mat.at[now], r_mat.at[3 - now])
            now = 3 - now
            d_row = [d * d for d in d_row]
            d_col = [d * d for d in d_col]


def kernel(
    tokens,
    damping,
    stats,
    grad,
    o_all,
    sbuf,
    native,
    tiles,
    acc,
    partner_in,
    y_out,
    y_in,
    z_out,
    packed,
    off_r,
    off_s,
    r_mat,
    s_mat,
    inverse,
    g_rows,
    g_buf,
    q_buf,
    q_sum,
    o_buf,
    stats_sem,
    local_sem,
    grad_send,
    grad_recv,
    part_send,
    part_recv,
    y_send,
    y_recv,
    z_send,
    x_send,
    x_recv,
    m_send,
    g_send,
    g_recv,
    out_send,
    out_recv,
    go,
):
    dp = lax.axis_index("dp")
    o = lax.axis_index("owner")
    h, c = dp // 2, dp % 2
    x, l, z = o % 4, (o // 4) % 2, o // 8
    quarter = W // 4
    half = W // 2

    def ring(t):
        return o - x + (x + t) % 4

    def y_place(step):
        y = (h * 2 + l + step) % 4
        return (y // 2) * 2 + c, z * 8 + (y % 2) * 4 + x

    def z_place(step):
        return dp, (o + 8 * step) % 32

    partner = (h * 2 + 1 - c, o)
    across = ((1 - h) * 2 + c, o)

    steps = sbuf.shape[1] // TOKEN_CHUNK

    def load(f, k):
        rows = pl.ds(k * TOKEN_CHUNK, TOKEN_CHUNK)
        return pltpu.make_async_copy(
            stats.at[f, rows], sbuf.at[f, rows], stats_sem.at[f * steps + k]
        )

    tiles_load = pltpu.make_async_copy(grad, native, local_sem.at[2])
    tiles_load.start()
    for f in range(2):
        for k in range(steps):
            load(f, k).start()
    mine = pl.ds(pl.multiple_of(dp * quarter, quarter), quarter)

    def own_tile(tau):
        return pltpu.make_async_copy(
            tiles.at[2 * c + tau], g_buf.at[tau, mine], local_sem.at[tau]
        )

    barrier = pltpu.get_barrier_semaphore()

    def greet(device):
        pl.semaphore_signal(barrier, inc=1, device_id=device, device_id_type=MESH)

    greet(partner)
    greet(across)
    greet(((1 - h) * 2 + 1 - c, o))

    @pl.when(c == 0)
    def _():
        greet((dp, ring(1)))
        greet((dp, ring(3)))
        greet((dp + 1, ring(2)))
        greet((dp + 1, ring(3)))
        for step in (1, 3):
            greet(y_place(step))
            greet(z_place(step))

    @pl.when(c == 1)
    def _():
        greet((dp - 1, ring(2)))
        greet((dp - 1, ring(1)))

    tiles_load.wait()
    tiles[...] = jnp.swapaxes(native[...], 0, 1)

    @pl.when(c == 0)
    def _():
        pl.semaphore_wait(barrier, 11)

    @pl.when(c == 1)
    def _():
        pl.semaphore_wait(barrier, 5)

    def grad_copy(rel, tau):
        to_h = h if rel < 2 else 1 - h
        to_c = c if rel % 2 == 0 else 1 - c
        n = (rel - 1) * 2 + tau
        return pltpu.make_async_remote_copy(
            src_ref=tiles.at[2 * to_c + tau],
            dst_ref=g_buf.at[tau, mine],
            send_sem=grad_send.at[n],
            recv_sem=grad_recv.at[n],
            device_id=(to_h * 2 + to_c, o),
            device_id_type=MESH,
        )

    def send_later_grads():
        grad_copy(3, 0).start()
        grad_copy(2, 1).start()
        grad_copy(3, 1).start()

    grad_copy(2, 0).start()
    for tau in range(2):
        own_tile(tau).start()

    def part_copy(k):
        rows = pl.ds(0, UPPER) if k == 0 else pl.ds(UPPER, TAIL - UPPER)
        return pltpu.make_async_remote_copy(
            src_ref=acc.at[1 - c, rows],
            dst_ref=partner_in.at[rows],
            send_sem=part_send.at[k],
            recv_sem=part_recv.at[k],
            device_id=partner,
            device_id_type=MESH,
        )

    def partial(f, _):
        for k in range(steps):
            load(f, k).wait()
            rows = slice(k * TOKEN_CHUNK, (k + 1) * TOKEN_CHUNK)
            for i in range(3):
                r = gram(sbuf[f, rows, i * N : (i + 1) * N], sbuf[f, rows, i * N :])
                for j in range(i, 3):
                    add_block(acc, f, i, j, r[:, (j - i) * N : (j - i + 1) * N], k == 0)

        @pl.when(f == 1 - c)
        def _():
            for k in range(2):
                part_copy(k).start()

        return 0

    lax.fori_loop(0, 2, partial, 0)
    grad_copy(1, 0).start()
    grad_copy(1, 1).start()
    bias = damping[c] * (0.5 * tokens)

    def sum_of_chip(k, diags):
        if k % 3 == 0:
            part_copy(k // 3).wait_recv()
        start, size = DATA[k]
        rows = slice(start, start + size)
        v = acc[c, rows, :] + partner_in[rows, :]
        acc[c, rows, :] = v
        y_out[rows, :] = v.astype(BF16)
        diags.extend(diagonals(k, v, bias))
        if k == 5:
            y_out[TAIL:ROWS, :] = pack_diagonal(diags)

    def y_copy(src, slot, device, k, send):
        start, size = CHUNKS[k]
        return pltpu.make_async_remote_copy(
            src_ref=src.at[pl.ds(start, size)],
            dst_ref=y_in.at[slot, pl.ds(start, size)],
            send_sem=y_send.at[send],
            recv_sem=y_recv.at[slot * 6 + k],
            device_id=device,
            device_id_type=MESH,
        )

    def y_plus(k):
        return y_copy(y_out, 0, y_place(1), k, k)

    def y_minus(k):
        return y_copy(y_out, 1, y_place(3), k, 6 + k)

    def y_on(k):
        if k < 3:
            return y_copy(y_in.at[0], 2, y_place(1), k, 12 + k)
        return y_copy(y_in.at[1], 2, y_place(3), k, 12 + k)

    def y_across(k):
        return y_copy(y_out, 2, across, k, k)

    def x_copy(t, k, slot):
        start, size = CHUNKS[k]
        to_slot = (1, 1, 2)[t - 1]
        return pltpu.make_async_remote_copy(
            src_ref=packed.at[slot, pl.ds(start, size)],
            dst_ref=packed.at[to_slot, pl.ds(start, size)],
            send_sem=x_send.at[(t - 1) * 6 + k],
            recv_sem=x_recv.at[to_slot * 6 + k],
            device_id=(dp + (0 if t == 1 else 1), ring(t)),
            device_id_type=MESH,
        )

    def z_copy(k):
        start, size = CHUNKS[k]
        return pltpu.make_async_remote_copy(
            src_ref=z_out.at[pl.ds(start, size)],
            dst_ref=packed.at[3, pl.ds(start, size)],
            send_sem=z_send.at[k],
            recv_sem=x_recv.at[18 + k],
            device_id=z_place(1),
            device_id_type=MESH,
        )

    def m_copy(k):
        start, size = CHUNKS[k]
        return pltpu.make_async_remote_copy(
            src_ref=packed.at[0, pl.ds(start, size)],
            dst_ref=packed.at[2, pl.ds(start, size)],
            send_sem=m_send.at[k],
            recv_sem=x_recv.at[12 + k],
            device_id=partner,
            device_id_type=MESH,
        )

    def sum_of_row(k, diags):
        start, size = DATA[k]
        rows = slice(start, start + size)
        packed[0, rows, :] = (acc[c, rows, :] + y_in[2, rows, :].astype(F32)).astype(BF16)
        if k == 5:
            other = unpack_diagonal(y_in[2, TAIL:ROWS, :])
            packed[0, TAIL:ROWS, :] = pack_diagonal([d + e for d, e in zip(diags, other)])

    def sum_of_other_row(k, dst):
        start, size = DATA[k]
        rows = slice(start, start + size)
        dst[rows, :] = (y_in[0, rows, :].astype(F32) + y_in[1, rows, :].astype(F32)).astype(BF16)
        if k == 5:
            one = unpack_diagonal(y_in[0, TAIL:ROWS, :])
            two = unpack_diagonal(y_in[1, TAIL:ROWS, :])
            dst[TAIL:ROWS, :] = pack_diagonal([d + e for d, e in zip(one, two)])

    def send_on(k, slot, ts):
        for t in ts:

            @pl.when((x + t < 4) if slot == 0 else (x + t >= 4))
            def _():
                x_copy(t, k, slot).start()

    @pl.when(c == 0)
    def _():
        diags = []
        for k in range(6):
            sum_of_chip(k, diags)
            if k < 3:
                y_plus(k).start()
            if k < 4:
                y_minus(k).start()

        def other_row(k):
            @pl.when(l == 0)
            def _():
                sum_of_other_row(k, z_out)
                z_copy(k).start()

            @pl.when(l == 1)
            def _():
                sum_of_other_row(k, packed.at[3])
                send_on(k, 3, (1, 2, 3))

        def from_z(k):
            @pl.when(l == 0)
            def _():
                z_copy(k).wait_recv()
                send_on(k, 3, (1, 2, 3))

        def own_row(k):
            y_on(k).wait_recv()
            sum_of_row(k, diags)
            send_on(k, 0, (1, 2, 3))

        for k in range(3):
            y_plus(k).wait_recv()
            y_on(k).start()
            y_plus(k + 3).start()
            y_minus(k).wait_recv()
            other_row(k)
            if k >= 2:
                from_z(k - 2)
        for k in range(3, 6):
            y_minus(k).wait_recv()
            y_on(k).start()
            if k < 5:
                y_minus(k + 1).start()
            if k == 4:
                pl.semaphore_signal(go, inc=1, device_id=partner, device_id_type=MESH)
            y_plus(k).wait_recv()
            other_row(k)
            from_z(k - 2)
            if k == 4:
                own_row(0)
        own_row(3)
        own_row(1)
        from_z(4)
        own_row(4)
        own_row(2)
        from_z(5)
        own_row(5)
        send_later_grads()
    @pl.when(c == 1)
    def _():
        diags = []
        for k in range(6):
            sum_of_chip(k, diags)
        pl.semaphore_wait(go, 1)
        for k in range(6):
            y_across(k).start()
        for k in range(6):
            y_across(k).wait_recv()
            sum_of_row(k, diags)
            m_copy(k).start()
        send_later_grads()

    g_copy = pltpu.make_async_remote_copy(
        src_ref=g_rows,
        dst_ref=g_rows,
        send_sem=g_send.at[0],
        recv_sem=g_recv.at[0],
        device_id=partner,
        device_id_type=MESH,
    )
    chip_rows = pl.ds(pl.multiple_of(h * half, half), half)
    far_rows = pl.ds(pl.multiple_of((1 - h) * half, half), half)

    def one(n, _):
        slot = (1 - c) * ((2 * n) % 3) + c * ((n + 1) % 3)

        @pl.when((c == 0) | (n < 2))
        def _():
            @pl.when(slot >= 1)
            def _():
                for k in range(6):
                    start, size = CHUNKS[k]
                    pltpu.make_async_remote_copy(
                        src_ref=packed.at[0, pl.ds(start, size)],
                        dst_ref=packed.at[1, pl.ds(start, size)],
                        send_sem=m_send.at[k],
                        recv_sem=x_recv.at[slot * 6 + k],
                        device_id=partner,
                        device_id_type=MESH,
                    ).wait_recv()

            invert(packed.at[slot], tokens, off_r, off_s, r_mat, s_mat, inverse.at[slot])

            @pl.when((c == 0) & (n == 1))
            def _():
                g_rows[...] = inverse[2, chip_rows, :]
                g_copy.start()

        return 0

    lax.fori_loop(0, 3, one, 0)

    @pl.when(c == 1)
    def _():
        g_copy.wait_recv()

    own_rows = pl.ds(pl.multiple_of(c * quarter, quarter), quarter)
    other_rows = pl.ds(pl.multiple_of((1 - c) * quarter, quarter), quarter)

    def out_copy(tau):
        return pltpu.make_async_remote_copy(
            src_ref=o_buf.at[tau],
            dst_ref=o_all.at[2 * c + tau],
            send_sem=out_send.at[tau],
            recv_sem=out_recv.at[tau],
            device_id=partner,
            device_id_type=MESH,
        )

    def tile(tau, _):
        own_tile(tau).wait()
        grad_copy(1, tau).wait_recv()
        q_sum[...] = jnp.dot(
            g_rows[:, chip_rows], g_buf[tau, chip_rows, :], preferred_element_type=F32
        )
        for rel in (2, 3):
            grad_copy(rel, tau).wait_recv()
        rest = jnp.dot(
            g_rows[:, far_rows], g_buf[tau, far_rows, :], preferred_element_type=F32
        )
        q_buf[...] = (q_sum[...] + rest).astype(BF16)
        a = inverse.at[tau + c]
        o_buf[tau] = jnp.dot(q_buf[other_rows, :], a[...], preferred_element_type=F32).astype(BF16)
        out_copy(tau).start()
        o_all[2 * c + tau] = jnp.dot(q_buf[own_rows, :], a[...], preferred_element_type=F32).astype(
            BF16
        )
        return 0

    lax.fori_loop(0, 2, tile, 0)

    for k in range(2):
        part_copy(k).wait_send()
    for rel in (1, 2, 3):
        for tau in range(2):
            grad_copy(rel, tau).wait_send()

    @pl.when(c == 1)
    def _():
        for k in range(6):
            y_across(k).wait_send()
            m_copy(k).wait_send()

    @pl.when(c == 0)
    def _():
        g_copy.wait_send()
        for k in range(6):
            y_plus(k).wait_send()
            y_minus(k).wait_send()
            y_on(k).wait_send()

            @pl.when(l == 0)
            def _():
                z_copy(k).wait_send()

            for t in range(1, 4):
                x_copy(t, k, 0).wait_send()

    for tau in range(2):
        out_copy(tau).wait()


def rows_first(by_tile, out):
    out[...] = jnp.swapaxes(by_tile[...], 0, 1)


def per_device(stats, damping, grad, total_tokens):
    local_tokens = stats.shape[2]
    quarter, band, width = grad.shape[1:]
    dma = pltpu.SemaphoreType.DMA
    result = pl.pallas_call(
        functools.partial(kernel, float(total_tokens)),
        out_shape=jax.ShapeDtypeStruct((band, quarter, width), BF16),
        in_specs=[
            pl.BlockSpec(memory_space=pltpu.SMEM),
            pl.BlockSpec(memory_space=pl.ANY),
            pl.BlockSpec(memory_space=pl.ANY),
        ],
        out_specs=pl.BlockSpec(memory_space=pltpu.VMEM),
        scratch_shapes=[
            pltpu.VMEM((2, local_tokens, width), BF16),
            pltpu.VMEM((quarter, band, width), BF16),
            pltpu.VMEM((band, quarter, width), BF16),
            pltpu.VMEM((2, TAIL, N), F32),
            pltpu.VMEM((TAIL, N), F32),
            pltpu.VMEM((ROWS, N), BF16),
            pltpu.VMEM((3, ROWS, N), BF16),
            pltpu.VMEM((ROWS, N), BF16),
            pltpu.VMEM((4, ROWS, N), BF16),
            pltpu.VMEM((6, N, N), F32),
            pltpu.VMEM((6, N, N), F32),
            pltpu.VMEM((3, W, W), BF16),
            pltpu.VMEM((2, W, W), BF16),
            pltpu.VMEM((3, W, W), BF16),
            pltpu.VMEM((W // 2, W), BF16),
            pltpu.VMEM((2, W, W), BF16),
            pltpu.VMEM((W // 2, W), BF16),
            pltpu.VMEM((W // 2, W), F32),
            pltpu.VMEM((2, W // 4, W), BF16),
            dma((2 * local_tokens // TOKEN_CHUNK,)),
            dma((3,)),
            dma((6,)),
            dma((6,)),
            dma((2,)),
            dma((2,)),
            dma((18,)),
            dma((18,)),
            dma((6,)),
            dma((18,)),
            dma((24,)),
            dma((6,)),
            dma((1,)),
            dma((1,)),
            dma((2,)),
            dma((2,)),
            pltpu.SemaphoreType.REGULAR,
        ],
        compiler_params=pltpu.CompilerParams(
            collective_id=0, has_side_effects=True, vmem_limit_bytes=56 * 2**20
        ),
    )(damping[0], stats[0], grad[0])
    return pl.pallas_call(
        rows_first,
        out_shape=jax.ShapeDtypeStruct((quarter, band, width), BF16),
        in_specs=[pl.BlockSpec(memory_space=pltpu.VMEM)],
        out_specs=pl.BlockSpec(memory_space=pltpu.VMEM),
    )(result)[None]


def solution(mesh):
    in_specs = (P("owner", None, "dp", None), P("owner", None), P("owner", "dp", None, None))
    out_specs = P("owner", "dp", None, None)

    def whole(stats, damping, grad):
        def one(s, d, g):
            return per_device(s, d, g, stats.shape[2])

        return jax.shard_map(
            one, mesh=mesh, in_specs=in_specs, out_specs=out_specs, check_vma=False
        )(stats, damping, grad)

    return whole
```
